32 devices in a mesh: seq: 4 (over x, core), dp: 8 (over z, y).
Axes of the slice: x: 2, y: 2, z: 4, core: 2. Of those that a mesh axis runs over, the one named last changes fastest.
Arguments:
- resid: bfloat16 [8, 4096, 768], P('dp', 'seq'), may hold values from -6 to 6
- cotangent: bfloat16 [8, 4096, 768], P('dp', 'seq'), may hold values from -6 to 6
- doc_lengths: int32 [8, 16], P('dp'), may hold values from 1 to 4081, as said below
- in_weight: float32 [768, 3352], P(('seq', 'dp')), may hold values from -0.21875 to 0.21875
- out_weight: float32 [1536, 768], P(('seq', 'dp')), may hold values from -0.15625 to 0.15625
- vec_params: float32 [11336], replicated, may hold values from -9 to 1.5, as said below
- in_moment: float32 [768, 3352], P(('seq', 'dp')), may hold values from -320 to 320
- out_moment: float32 [1536, 768], P(('seq', 'dp')), may hold values from -1024 to 1024
- vec_first: float32 [11336], replicated, may hold values from -32 to 32
- vec_second: float32 [11336], replicated, may hold values from 163.84 to 655.36
Outputs:
- block_out: bfloat16 [8, 4096, 768], P('dp', 'seq')
- input_grad: float32 [8, 4096, 768], P('dp', 'seq')
- in_moment_new: float32 [768, 3352], P(('seq', 'dp'))
- in_weight_new: float32 [768, 3352], P(('seq', 'dp'))
- out_moment_new: float32 [1536, 768], P(('seq', 'dp'))
- out_weight_new: float32 [1536, 768], P(('seq', 'dp'))
- vec_first_new: float32 [11336], replicated
- vec_second_new: float32 [11336], replicated
- vec_params_new: float32 [11336], replicated
The draws below stay inside these ranges and needn't reach their ends.
Inputs may be any that keep to these rules, and one draw needn't show every extreme that they name: `doc_lengths`: each row holds 16 document lengths that sum to 4096. In some rows (at least one) one document, at a place drawn from the seed, starts within the first 1024 tokens and ends within the last 1024; in the other rows (at least one) two neighbouring documents, at a place drawn from the seed, meet exactly at token 2048, the first starting within the first 1024 tokens and the second ending within the last 1024. Every other document has at most 64 tokens. `vec_params`: gains lie in 0.5 to 1.5; the step bias is the inverse softplus of a step size between 0.0002 and 0.05; exp(a_log) lies in 1 to 2.
All inputs are finite; a program needn't handle non-finite values.
Results may differ from the reference program's by a relative error of at most 0.011.
Values may be sent and summed in bfloat16 or wider, within the bound.
No kernel may reach another device: no remote copies, remote signals or barrier semaphores. Data moves between devices by JAX's collectives and lax.ppermute only.
A program may use at most 192 MiB of HBM per device.

```python
import math
import jax
import jax.numpy as jnp
from jax import lax

D = 768
INNER = 1536
HEADDIM = 64
NSTATE = 128
CONV = 4
BLOCK = 256
SWEEPS = 5
STEP = 10
DOCS = 16
LEN_DEV = 1024
HEADS = 24
XBC = 1792
PROJ = 3352
VEC = 11336
LEN = 4096
SEQS = 8
N_SEQ = 4
N_DP = 8


def draw_doc_lengths(key, part):
    key = jax.random.fold_in(key, 23)
    key_short, key_which, key_row, key_mode, key_pair, key_split = jax.random.split(key, 6)
    shorts = jax.random.randint(key_short, (SEQS, DOCS), 1, LEN_DEV // DOCS + 1)
    row_index = jnp.arange(SEQS)[:, None]
    picked_row = jax.random.randint(key_row, (1, 1), 0, SEQS)
    shorts = jnp.where(row_index == picked_row, 1, shorts)
    split_row = (picked_row + 1 + jax.random.randint(key_split, (1, 1), 0, SEQS - 1)) % SEQS
    halved = (jax.random.randint(key_mode, (SEQS, 1), 0, 4) == 0) | (row_index == split_row)
    halved = halved & (row_index != picked_row)
    column = jnp.arange(DOCS)[None, :]
    which = jax.random.randint(key_which, (SEQS, 1), 0, DOCS)
    is_long = column == which
    others = jnp.sum(jnp.where(is_long, 0, shorts), axis=1, keepdims=True)
    one_long = jnp.where(is_long, LEN - others, shorts)
    pair = jax.random.randint(key_pair, (SEQS, 1), 0, DOCS - 1)
    before_sum = jnp.sum(jnp.where(column < pair, shorts, 0), axis=1, keepdims=True)
    after_sum = jnp.sum(jnp.where(column > pair + 1, shorts, 0), axis=1, keepdims=True)
    two_long = jnp.where(column == pair, LEN // 2 - before_sum, jnp.where(column == pair + 1, LEN - LEN // 2 - after_sum, shorts))
    return jnp.where(halved, two_long, one_long).astype(jnp.int32)


def draw_vec_params(key, part):
    key = jax.random.fold_in(key, 11)
    keys = jax.random.split(key, 7)
    gain_in = jax.random.uniform(keys[0], (D,), jnp.float32, 0.5, 1.5)
    gain_norm = jax.random.uniform(keys[1], (INNER,), jnp.float32, 0.5, 1.5)
    conv_taps = jax.random.uniform(keys[2], (CONV * XBC,), jnp.float32, -0.9, 0.9)
    conv_bias = jax.random.uniform(keys[3], (XBC,), jnp.float32, -0.5, 0.5)
    low_step = 0.0005
    high_step = 0.05
    step_init = jnp.exp(jax.random.uniform(keys[4], (HEADS,), jnp.float32, jnp.log(low_step), jnp.log(high_step)))
    dt_bias = jnp.log(jnp.expm1(step_init))
    a_log = jnp.log(jax.random.uniform(keys[5], (HEADS,), jnp.float32, 1.0, 2.0))
    d_skip = jax.random.uniform(keys[6], (HEADS,), jnp.float32, -1.5, 1.5)
    return jnp.concatenate([gain_in, gain_norm, conv_taps, conv_bias, dt_bias, a_log, d_skip]).astype(jnp.float32)


def steps_of(key, dims, shards, low, largest):
    factor_of = 1.0
    for position, parts in shards:
        steps = jax.random.uniform(jax.random.fold_in(jax.random.fold_in(key, 6), position), (parts,), jnp.float32, low / len(shards), largest / len(shards))
        factor_of = factor_of * jnp.repeat(jnp.exp(steps), dims[position] // parts).reshape((-1,) + (1,) * (len(dims) - 1 - position))
    return factor_of


def noise(key, extent, deviation, reach, cuts=(), dtype=jnp.bfloat16):
    values = jax.random.normal(key, extent, jnp.float32) * deviation
    if len(cuts) > 0:
        values = steps_of(key, extent, cuts, -0.22, 0.18) * values
    return jnp.clip(values, min=-reach, max=reach).astype(dtype)


def setup_inputs(seed: int = 0) -> dict:
    splits = jax.random.split(jax.random.key(seed), 11)
    return {
        "resid": noise(splits[0], (SEQS, LEN, D), 1.0, 6.0, ((0, 8), (1, 4))),
        "cotangent": noise(splits[1], (SEQS, LEN, D), 1.0, 6.0, ((0, 8), (1, 4))),
        "doc_lengths": draw_doc_lengths(jax.random.fold_in(splits[10], 71), 0),
        "in_weight": noise(splits[3], (D, PROJ), D ** -0.5, 0.21875, ((0, 32),), jnp.float32),
        "out_weight": noise(splits[4], (INNER, D), INNER ** -0.5, 0.15625, ((0, 32),), jnp.float32),
        "vec_params": draw_vec_params(jax.random.fold_in(splits[10], 71), 0),
        "in_moment": noise(splits[6], (D, PROJ), (0.3 * (LEN_DEV * N_SEQ * N_DP) ** 0.5), 320.0, ((0, 32),), jnp.float32),
        "out_moment": noise(splits[7], (INNER, D), ((LEN_DEV * N_SEQ * N_DP) ** 0.5), 1024.0, ((0, 32),), jnp.float32),
        "vec_first": noise(splits[8], (VEC,), (0.03 * (LEN_DEV * N_SEQ * N_DP) ** 0.5), 32.0, (), jnp.float32),
        "vec_second": jnp.clip(jnp.exp(jax.random.uniform(splits[9], (VEC,), jnp.float32, math.log(163.84), math.log(655.36))), 163.84, 655.36),
    }


highest = lax.Precision.HIGHEST
norm_eps = 1e-05
ortho_eps = 1e-07
schulz_coef = (3.4445, -4.775, 2.0315)
moment_decay = 0.95
muon_rate = 0.5
muon_shrink = 0.01
adam_first = 0.9
adam_second = 0.95
adam_rate = 0.2
adam_eps = 1e-08

@jax.custom_vjp
def low(v):
    return lax.optimization_barrier(v.astype(jnp.bfloat16)).astype(jnp.float32)

@jax.custom_vjp
def low_back(v):
    return v

def low_keep(v):
    return (low(v), None)

def low_pass(kept, grad):
    return (grad,)

def back_keep(v):
    return (v, None)

def back_low(kept, grad):
    return (low(grad),)
low.defvjp(low_keep, low_pass)
low_back.defvjp(back_keep, back_low)

def split_vector(vector):
    spans = (D, INNER, CONV * XBC, XBC, HEADS, HEADS, HEADS)
    pieces = []
    offset = 0
    for span_size in spans:
        pieces.append(vector[offset:offset + span_size])
        offset = offset + span_size
    gain_in, gain_norm, conv_taps, conv_bias, dt_bias, a_log, d_skip = pieces
    return (gain_in, gain_norm, conv_taps.reshape(CONV, XBC), conv_bias, dt_bias, a_log, d_skip)

def segment_of(lengths, positions):
    doc_ends = jnp.cumsum(lengths)
    counted = (doc_ends[None, :] <= positions[:, None]).astype(jnp.int32)
    return jnp.where(positions < 0, -1, lax.optimization_barrier(jnp.sum(counted, axis=1))).astype(jnp.int32)

def conv_masks(seg_ext, segment):
    tok_count = segment.shape[0]
    return jnp.stack([(seg_ext[tap_index:tap_index + tok_count] == segment).astype(jnp.float32)[:, None] for tap_index in range(CONV)])

def prepare(xbc_ext, dt_raw, conv_taps, conv_bias, dt_bias, a_log, same_ext):
    tok_count = dt_raw.shape[0]
    summed = conv_bias[None, :]
    for tap_index in range(CONV):
        summed = summed + conv_taps[tap_index][None, :] * xbc_ext[tap_index:tap_index + tok_count] * same_ext[tap_index]
    activated = jax.nn.silu(summed)
    head_x = activated[:, :INNER].reshape(tok_count, HEADS, HEADDIM)
    b_proj = activated[:, INNER:INNER + NSTATE]
    c_proj = activated[:, INNER + NSTATE:]
    step_size = jax.nn.softplus(dt_raw + dt_bias[None, :])
    log_decay = -step_size * jnp.exp(a_log)[None, :]
    return (head_x, b_proj, c_proj, log_decay, step_size)

def block_end(state_in, head_x, b_proj, log_decay, step_size, segment, before):
    cum_decay = jnp.cumsum(log_decay, axis=0)
    carried = (segment[-1] == before).astype(jnp.float32) * jnp.exp(cum_decay[-1])
    kept = (segment == segment[-1]).astype(jnp.float32)[:, None] * jnp.exp(cum_decay[-1][None, :] - cum_decay) * step_size
    return carried[:, None, None] * state_in + jnp.einsum('sh,shp,sn->hpn', kept, head_x, b_proj, precision=highest)

def block_mix(state_in, pieces):
    head_x, b_proj, c_proj, log_decay, step_size, segment, before = pieces
    block_len = segment.shape[0]
    cum_decay = jnp.cumsum(log_decay, axis=0)
    order = jnp.arange(block_len)
    same = (segment[:, None] == segment[None, :]) & (order[:, None] >= order[None, :])
    spread = jnp.where(same[:, :, None], cum_decay[:, None, :] - cum_decay[None, :, :], 0.0)
    decays = jnp.where(same[:, :, None], jnp.exp(spread), 0.0)
    scores = jnp.dot(c_proj, b_proj.T, precision=highest)
    weights = decays * scores[:, :, None] * step_size[None, :, :]
    mixed = jnp.einsum('tsh,shp->thp', weights, head_x, precision=highest)
    lead = (segment == before).astype(jnp.float32)[:, None] * jnp.exp(cum_decay)
    mixed = mixed + lead[:, :, None] * jnp.einsum('hpn,tn->thp', state_in, c_proj, precision=highest)
    return (block_end(state_in, head_x, b_proj, log_decay, step_size, segment, before), mixed)

def block_befores(segment, before):
    return jnp.concatenate([jnp.reshape(before, (1,)), segment[BLOCK - 1::BLOCK][:-1]]).astype(jnp.int32)

def run_blocks(head_x, b_proj, c_proj, log_decay, step_size, d_skip, state_in, segment, before):
    tok_count = segment.shape[0]
    blocks = tok_count // BLOCK
    pieces = (head_x.reshape(blocks, BLOCK, HEADS, HEADDIM), b_proj.reshape(blocks, BLOCK, NSTATE), c_proj.reshape(blocks, BLOCK, NSTATE), log_decay.reshape(blocks, BLOCK, HEADS), step_size.reshape(blocks, BLOCK, HEADS), segment.reshape(blocks, BLOCK), block_befores(segment, before))
    state_end, mixed = lax.scan(jax.checkpoint(block_mix), state_in, pieces)
    mixed = mixed.reshape(tok_count, HEADS, HEADDIM) + d_skip[None, :, None] * head_x
    return (mixed.reshape(tok_count, INNER), state_end)

def in_norm(resid, gain_in):
    return resid * lax.rsqrt(lax.optimization_barrier(jnp.mean(resid * resid, axis=-1, keepdims=True)) + norm_eps) * gain_in[None, :]

def gate_norm(mixed, gate, gain_norm):
    value = mixed * jax.nn.silu(gate)
    return value * lax.rsqrt(lax.optimization_barrier(jnp.mean(value * value, axis=-1, keepdims=True)) + norm_eps) * gain_norm[None, :]

def forward(resid, in_weight, out_weight, vector, segment):
    gain_in, gain_norm, conv_taps, conv_bias, dt_bias, a_log, d_skip = split_vector(vector)
    normed = low(in_norm(resid, gain_in))
    proj = low_back(low(jnp.dot(normed, low(in_weight), precision=highest)))
    gate = proj[:, :INNER]
    xbc = proj[:, INNER:INNER + XBC]
    dt_raw = proj[:, INNER + XBC:]
    xbc_ext = jnp.concatenate([jnp.zeros((CONV - 1, XBC), jnp.float32), xbc], axis=0)
    seg_ext = jnp.concatenate([jnp.full((CONV - 1,), -1, jnp.int32), segment]).astype(jnp.int32)
    same_ext = conv_masks(seg_ext, segment)
    head_x, b_proj, c_proj, log_decay, step_size = prepare(xbc_ext, dt_raw, conv_taps, conv_bias, dt_bias, a_log, same_ext)
    empty_state = jnp.zeros((HEADS, HEADDIM, NSTATE), jnp.float32)
    mixed, _ = run_blocks(head_x, b_proj, c_proj, log_decay, step_size, d_skip, empty_state, segment, jnp.array(-1, jnp.int32))
    gated = low(gate_norm(mixed, gate, gain_norm))
    return resid + jnp.dot(gated, low(out_weight), precision=highest)

def orthogonalize(matrix):
    current = matrix / (jnp.sqrt(jnp.sum(matrix * matrix)) + ortho_eps)
    for sweep_index in range(SWEEPS):
        gram_mat = jnp.dot(current, current.T, precision=highest)
        polynom = schulz_coef[1] * gram_mat + schulz_coef[2] * jnp.dot(gram_mat, gram_mat, precision=highest)
        current = schulz_coef[0] * current + jnp.dot(polynom, current, precision=highest)
    return current

def reference(resid, cotangent, doc_lengths, in_weight, out_weight, vec_params, in_moment, out_moment, vec_first, vec_second):
    positions = jnp.arange(LEN).astype(jnp.int32)
    segments = jax.vmap(lambda lengths: segment_of(lengths, positions))(doc_lengths)

    def one_sequence(totals, pieces):
        seq_resid, seq_cot, segment = pieces

        def closed(res_in, weight_in, weight_out, vector):
            return forward(res_in, weight_in, weight_out, vector, segment)
        result, pullback = jax.vjp(closed, seq_resid.astype(jnp.float32), in_weight, out_weight, vec_params)
        grad_resid, grad_in, grad_out, grad_vec = pullback(seq_cot.astype(jnp.float32))
        totals = (totals[0] + grad_in, totals[1] + grad_out, totals[2] + grad_vec)
        return (totals, (result.astype(jnp.bfloat16), grad_resid))
    start = (jnp.zeros_like(in_weight), jnp.zeros_like(out_weight), jnp.zeros_like(vec_params))
    (grad_in, grad_out, grad_vec), (block_out, input_grad) = lax.scan(one_sequence, start, (resid, cotangent, segments))
    in_moment_new = moment_decay * in_moment + grad_in
    out_moment_new = moment_decay * out_moment + grad_out
    in_orth = orthogonalize(in_moment_new)
    out_orth = orthogonalize(out_moment_new.T).T
    in_weight_new = in_weight * (1.0 - muon_rate * muon_shrink) - muon_rate * math.sqrt(PROJ / D) * in_orth
    out_weight_new = out_weight * (1.0 - muon_rate * muon_shrink) - muon_rate * out_orth
    first_new = adam_first * vec_first + (1.0 - adam_first) * grad_vec
    second_new = adam_second * vec_second + (1.0 - adam_second) * grad_vec * grad_vec
    first_hat = first_new / (1.0 - adam_first ** STEP)
    second_hat = second_new / (1.0 - adam_second ** STEP)
    params_new = vec_params - adam_rate * first_hat / (jnp.sqrt(second_hat) + adam_eps)
    return (block_out, input_grad, in_moment_new, in_weight_new, out_moment_new, out_weight_new, first_new, second_new, params_new)
```

```python
import functools
import math

import jax
import jax.numpy as jnp
from jax import lax
from jax.experimental import pallas as pl
from jax.experimental.pallas import tpu as pltpu
from jax.sharding import PartitionSpec as P

D = 768
INNER = 1536
HEADDIM = 64
NSTATE = 128
CONV = 4
SWEEPS = 5
STEP = 10
HEADS = 24
XBC = 1792
PROJ = 3352
VEC = 11336


norm_eps = 1e-05
ortho_eps = 1e-07
schulz_coef = (3.4445, -4.775, 2.0315)
moment_decay = 0.95
muon_rate = 0.5
muon_shrink = 0.01
adam_first = 0.9
adam_second = 0.95
adam_rate = 0.2
adam_eps = 1e-08


CHUNK = 128
LANES = 128
WIDE = 256
SPLIT = 1920
LOG2E = 1.4426950408889634
f32 = jnp.float32
bf16 = jnp.bfloat16


def passed_along(block, axis, distance):
    devices = range(lax.axis_size(axis))
    route = [(i - distance, i) for i in devices if i - distance in devices]
    return lax.ppermute(block, axis, route)


def split_vector(vector):
    spans = (D, INNER, CONV * XBC, XBC, HEADS, HEADS, HEADS)
    pieces = []
    offset = 0
    for span_size in spans:
        pieces.append(vector[offset : offset + span_size])
        offset = offset + span_size
    gain_in, gain_norm, conv_taps, conv_bias, dt_bias, a_log, d_skip = pieces
    return (gain_in, gain_norm, conv_taps.reshape(CONV, XBC), conv_bias, dt_bias, a_log, d_skip)


def in_norm(resid, gain_in):
    return (
        resid
        * lax.rsqrt(jnp.mean(resid * resid, axis=-1, keepdims=True) + norm_eps)
        * gain_in[None, :]
    )


def mm(a, b):
    return lax.dot_general(a, b, (((1,), (0,)), ((), ())), preferred_element_type=f32)


def mm_nt(a, b):
    return lax.dot_general(a, b, (((1,), (1,)), ((), ())), preferred_element_type=f32)


def mm_tn(a, b):
    return lax.dot_general(a, b, (((0,), (0,)), ((), ())), preferred_element_type=f32)


def iota(shape, dim):
    return lax.broadcasted_iota(jnp.int32, shape, dim)


def sigmoid(v):
    return 0.5 * jnp.tanh(0.5 * v) + 0.5


def setup_kernel(
    docs_ref, vec_ref,
    start_ref, row_ref, spread_ref, gather_ref, taps_ref, bias_ref, heads_ref, skip_ref, gain_ref, gain_in_ref,
):
    def starts(pos):
        start = jnp.zeros_like(pos)
        end = 0
        for j in range(docs_ref.shape[0] - 1):
            end = end + docs_ref[j + 1]
            start = jnp.maximum(start, jnp.where(pos >= end, end, 0))
        return start

    start_ref[...] = starts(docs_ref[0] + iota(start_ref.shape, 0))
    row_ref[...] = starts(docs_ref[0] + iota(row_ref.shape, 1))
    row, head = iota(spread_ref.shape, 0), iota(spread_ref.shape, 1) >> 6
    spread_ref[...] = ((row == head) | (row == head + HEADS)).astype(bf16)
    gather_ref[...] = (iota(gather_ref.shape, 1) == iota(gather_ref.shape, 0) >> 6).astype(bf16)
    at = 0
    for ref in (gain_in_ref, gain_ref):
        ref[...] = vec_ref[:, at : at + ref.shape[1]]
        at = at + ref.shape[1]
    for k in range(CONV):
        taps_ref[k : k + 1, :] = vec_ref[:, at : at + XBC]
        at = at + XBC
    bias_ref[...] = vec_ref[:, at : at + XBC]
    at = at + XBC
    rest = jnp.concatenate([vec_ref[:, at:], jnp.zeros((1, LANES - 3 * HEADS), f32)], axis=1)
    rows = jnp.broadcast_to(rest, (8, LANES))
    inside = iota((8, LANES), 1) < HEADS
    parts = [jnp.where(inside, pltpu.roll(rows, (LANES - k * HEADS) % LANES, 1), 0.0) for k in range(3)]
    which = iota((8, LANES), 0)
    rate = jnp.where(inside, jnp.exp(parts[1]), 0.0)
    heads_ref[...] = jnp.where(which == 0, parts[0], jnp.where(which == 1, rate, jnp.where(which == 2, parts[2], 0.0)))
    first = parts[2].astype(bf16).astype(f32)
    second = (parts[2] - first).astype(bf16).astype(f32)
    third = parts[2] - first - second
    wide = sum(mm(part.astype(bf16), spread_ref[...]) for part in (first, second, third))
    skip_ref[...] = wide[0:1, :]


def three_parts(v):
    first = v.astype(bf16).astype(f32)
    rest = v - first
    second = rest.astype(bf16).astype(f32)
    third = rest - second
    return (first + pltpu.roll(second, HEADS, 1) + pltpu.roll(third, 2 * HEADS, 1)).astype(bf16)


def three_sum(v):
    total = v + pltpu.roll(v, LANES - HEADS, 1) + pltpu.roll(v, LANES - 2 * HEADS, 1)
    return jnp.where(iota(v.shape, 1) < HEADS, total, 0.0)


def two_parts(v):
    v = jnp.where(iota(v.shape, 1) < HEADS, v, 0.0)
    first = v.astype(bf16).astype(f32)
    return (first + pltpu.roll(v - first, HEADS, 1)).astype(bf16)


def spread_matrix(first, width):
    row = iota((LANES, width), 0)
    head = (iota((LANES, width), 1) + first) >> 6
    return ((row == head) | (row == head + HEADS)).astype(bf16)


def gather_matrix(first, width):
    head = (iota((width, LANES), 0) + first) >> 6
    return (iota((width, LANES), 1) == head).astype(bf16)


def head_sum(v, gather):
    first = v.astype(bf16)
    return mm(first, gather) + mm((v - first.astype(f32)).astype(bf16), gather)


def conv_shifts(start, c0):
    rows = (CHUNK, CHUNK + 16)
    t = iota(rows, 0)
    j = iota(rows, 1)
    inside = c0 - 16 + j >= jnp.concatenate([start, start[:, :16]], axis=1)
    return [((j == t + 13 + k) & inside).astype(bf16) for k in range(3)]


def tri(lower):
    a, b = (iota((CHUNK, CHUNK), 0), iota((CHUNK, CHUNK), 1))
    return ((a >= b) if lower else (a <= b)).astype(bf16)


def decay_terms(start, c0, cum):
    pos = iota((CHUNK, LANES), 0) + c0
    start_end = start[CHUNK - 1 :, :]
    end = cum[CHUNK - 1 :, :]
    lead = jnp.where(start <= c0 - 1, jnp.exp(cum), 0.0)
    kept = jnp.where(pos >= start_end, jnp.exp(end - cum), 0.0)
    carried = jnp.where(start_end <= c0 - 1, jnp.exp(end), 0.0)
    return lead, kept, carried


def states_kernel(
    place_ref, start_ref, spread_ref, xbc_ref, halo_ref, taps_ref, bias_ref, heads_ref,
    act_ref, slope_ref, cum_ref, step_ref, lead_ref, begin_ref, factor_ref, end_ref,
    state, total,
):
    i = pl.program_id(0)
    c0 = place_ref[0] + i * CHUNK
    start = start_ref[...]

    @pl.when(i == 0)
    def _():
        state[...] = jnp.zeros_like(state)
        total[...] = jnp.ones_like(total)

    dt = xbc_ref[:, XBC:].astype(f32) + heads_ref[0:1, :]
    step = jnp.maximum(dt, 0.0) + jnp.log1p(jnp.exp(-jnp.abs(dt)))
    step = jnp.where(iota(step.shape, 1) < HEADS, step, 0.0)
    log_decay = -step * heads_ref[1:2, :]
    cum = three_sum(mm(tri(True), three_parts(log_decay)))
    cum_ref[...] = cum
    step_ref[...] = step
    lead, kept, carried = decay_terms(start, c0, cum)
    before = total[0:1, :]
    lead_ref[...] = lead * before
    after = before * carried
    total[...] = jnp.broadcast_to(after, total.shape)
    kept_two = two_parts(kept * step)
    rows = jnp.where(iota((16, LANES), 0) < 8, carried, before)
    factors = two_parts(rows)
    afters = two_parts(jnp.broadcast_to(after, (16, LANES)))
    shifts = conv_shifts(start, c0)

    def conv(first):
        cols = slice(first, first + WIDE)
        x = xbc_ref[:, cols]
        ext = jnp.concatenate([halo_ref[:, cols], x], axis=0)
        summed = bias_ref[:, cols] + taps_ref[0:1, cols] * mm(shifts[0], ext)
        summed = summed + taps_ref[1:2, cols] * mm(shifts[1], ext)
        summed = summed + taps_ref[2:3, cols] * mm(shifts[2], ext)
        summed = summed + taps_ref[3:4, cols] * x.astype(f32)
        sig = sigmoid(summed)
        value = summed * sig
        act_ref[:, cols] = value.astype(bf16)
        slope_ref[:, cols] = (sig + value * (1.0 - sig)).astype(bf16)
        return value

    b_turned = conv(INNER)[:, :NSTATE].T.astype(bf16)
    for first in range(0, INNER, WIDE):
        cols = slice(first, first + WIDE)
        x = conv(first)
        spread = spread_ref[:, cols]
        scaled = (x * mm(kept_two, spread)).astype(bf16)
        old = state[:, cols]
        begin_ref[0, :, cols] = old.astype(bf16)
        wide = mm(factors, spread)
        factor_ref[0, :, cols] = wide[8:16, :]
        new = wide[0:1, :] * old + mm(b_turned, scaled)
        state[:, cols] = new
        end_ref[0:NSTATE, cols] = new.astype(bf16)
        last = mm(afters, spread)
        coarse = last.astype(bf16)
        fine = (last - coarse.astype(f32)).astype(bf16)
        end_ref[NSTATE:, cols] = jnp.where(iota((16, WIDE), 0) == 0, coarse, fine)


def mix_kernel(place_ref, start_ref, spread_ref, act_ref, cum_ref, step_ref, begin_ref, skip_ref, mixed_ref):
    c0 = place_ref[0] + pl.program_id(0) * CHUNK
    cum = cum_ref[...]
    start = start_ref[...]
    lead, _, _ = decay_terms(start, c0, cum)
    b = act_ref[:, INNER : INNER + NSTATE]
    c = act_ref[:, INNER + NSTATE :]
    at = iota((CHUNK, CHUNK), 1)
    same = (c0 + at >= start) & (at <= iota((CHUNK, CHUNK), 0))
    scores = jnp.where(same, mm_nt(c, b), 0.0)
    log2 = cum * LOG2E
    log2_turned = log2.T
    step_two = two_parts(step_ref[...])
    lead_two = two_parts(lead)
    low_half = iota((CHUNK, LANES), 1) < HEADDIM

    def weight(head):
        gap = log2[:, head : head + 1] - log2_turned[head : head + 1, :]
        return (jnp.exp2(jnp.minimum(gap, 0.0)) * scores).astype(bf16)

    for first in range(0, INNER, WIDE):
        cols = slice(first, first + WIDE)
        spread = spread_ref[:, cols]
        x = act_ref[:, cols].astype(f32)
        stepped = (x * mm(step_two, spread)).astype(bf16)
        rest = mm(lead_two, spread) * mm(c, begin_ref[0, :, cols]) + skip_ref[:, cols] * x
        for part in range(2):
            head = first // HEADDIM + 2 * part
            half = slice(part * LANES, (part + 1) * LANES)
            pair = stepped[:, half]
            zero = jnp.zeros_like(pair)
            blocks = jnp.concatenate(
                [jnp.where(low_half, pair, zero), jnp.where(low_half, zero, pair)], axis=0
            )
            weights = jnp.concatenate([weight(head), weight(head + 1)], axis=1)
            mixed_ref[:, first + part * LANES : first + (part + 1) * LANES] = (
                mm(weights, blocks) + rest[:, half]
            )


def gate_kernel(
    order_ref, mixed_ref, gate_ref, c_ref, lead_ref, enter_ref, resid_ref, cot_ref, top_ref, bottom_ref, gain_ref,
    out_ref, gmixed_ref, ggate_ref, rows_ref, own_ref, other_ref, gstate_ref, ggain_ref,
    mixed, value, slope, back, state_sum, weight_sum, weight_ref,
):
    i = pl.program_id(0)
    last = pl.num_programs(0) - 1
    blocks = order_ref.shape[0]
    rows = D // blocks
    placed = rows % 8 == 0

    @pl.when(i == 0)
    def _():
        for j in range(blocks if placed else 0):
            at = slice(j * rows, (j + 1) * rows)
            block = jnp.concatenate([top_ref[at, :].astype(f32), bottom_ref[at, :].astype(f32)], axis=0)
            weight_ref[pl.ds(pl.multiple_of(order_ref[j] * (2 * rows), 2 * rows), 2 * rows), :] = block.astype(bf16)
        if not placed:
            weight_ref[...] = jnp.concatenate([top_ref[...], bottom_ref[...]], axis=0)
        state_sum[...] = jnp.zeros_like(state_sum)
        weight_sum[...] = jnp.zeros_like(weight_sum)
        ggain_ref[...] = jnp.zeros_like(ggain_ref)

    tokens = mixed_ref.shape[0]
    c = c_ref[...]
    cot = cot_ref[...]
    lead_two = two_parts(lead_ref[...])
    square = jnp.zeros((tokens, LANES), f32)
    for first in range(0, INNER, WIDE):
        cols = slice(first, first + WIDE)
        lead = mm(lead_two, spread_matrix(first, WIDE))
        whole = mixed_ref[:, cols] + lead * mm(c, enter_ref[:, cols])
        gate = gate_ref[:, cols].astype(f32)
        v = whole * (gate * sigmoid(gate))
        mixed[:, cols] = whole
        value[:, cols] = v
        vv = v * v
        square = square + vv[:, :LANES] + vv[:, LANES:]
    scale = lax.rsqrt(jnp.sum(square, axis=1, keepdims=True) * (1.0 / INNER) + norm_eps)
    along = jnp.zeros((tokens, LANES), f32)
    for first in range(0, INNER, WIDE):
        cols = slice(first, first + WIDE)
        v = value[:, cols] * scale
        gain = gain_ref[:, cols]
        slope[:, cols] = (v * gain).astype(bf16)
        g = mm_nt(cot, weight_ref[cols, :])
        gv = g * v
        ggain_ref[:, cols] += jnp.sum(gv.reshape(tokens // 8, 8, WIDE), axis=0)
        back[:, cols] = g * gain
        value[:, cols] = v
        gv = gv * gain
        along = along + gv[:, :LANES] + gv[:, LANES:]
    mean = jnp.sum(along, axis=1, keepdims=True) * (1.0 / INNER)
    gated = slope[...]
    out_ref[...] = (resid_ref[...].astype(f32) + mm(gated, weight_ref[...])).astype(bf16)
    weight_sum[...] += mm_tn(gated, cot)
    head_rows = jnp.zeros((tokens, LANES), f32)
    for first in range(0, INNER, WIDE):
        cols = slice(first, first + WIDE)
        gate = gate_ref[:, cols].astype(f32)
        sig = sigmoid(gate)
        silu = gate * sig
        gv = scale * (back[:, cols] - value[:, cols] * mean)
        whole = mixed[:, cols]
        gm = gv * silu
        gm_low = gm.astype(bf16)
        gmixed_ref[:, cols] = gm_low
        ggate_ref[:, cols] = (gv * whole * (sig + silu * (1.0 - sig))).astype(bf16)
        head_rows = head_rows + head_sum(gm_low.astype(f32) * whole, gather_matrix(first, WIDE))
        lead = mm(lead_two, spread_matrix(first, WIDE))
        state_sum[:, cols] += mm_tn(c, (lead * gm).astype(bf16))
    rows_ref[...] = head_rows

    @pl.when(i == last)
    def _():
        for j in range(0, blocks if placed else 0, 2):
            picked = [
                weight_sum[pl.ds(pl.multiple_of(order_ref[j + e] * (2 * rows), 2 * rows), 2 * rows), :]
                for e in range(2)
            ]
            target = own_ref if j < blocks // 2 else other_ref
            at = j % (blocks // 2) * rows
            for part in range(2):
                block = jnp.concatenate([p[part * rows : (part + 1) * rows] for p in picked], axis=0)
                target[at : at + 2 * rows, part * D : (part + 1) * D] = block.astype(bf16)
        if not placed:
            for part, target in enumerate((own_ref, other_ref)):
                for side in range(2):
                    at = side * D + part * (D // 2)
                    target[:, side * D : (side + 1) * D] = weight_sum[at : at + D // 2, :].astype(bf16)
        gstate_ref[...] = state_sum[...].astype(bf16)


def back_kernel(
    part, edge, place_ref, start_ref, row_ref, row_next_ref, spread_ref, gather_ref, xbc_ref, halo_ref, act_ref, slope_ref, cum_ref, step_ref, rows_ref, gm_ref,
    begin_ref, factor_ref, enter_ref, taps_ref, heads_ref, skip_ref, adjoint_in, later_in, carry_in, *refs,
):
    (gxbc_ref, gtaps_ref, gbias_ref, gheads_ref, adjoint_out, later_out, carry_out,
     adjoint, later, conv_rows, dx) = refs[-11:]
    i = pl.program_id(0)
    last = pl.num_programs(0) - 1
    chunks = pl.num_programs(0) - (1 if edge else 0)
    c0 = place_ref[0] + (part - 1 - i) * CHUNK
    start = start_ref[...]

    @pl.when(i == 0)
    def _():
        adjoint[...] = adjoint_in[...]
        later[...] = later_in[...]
        conv_rows[0:16, :] = carry_in[...]
        gtaps_ref[...] = jnp.zeros_like(gtaps_ref)
        gbias_ref[...] = jnp.zeros_like(gbias_ref)
        gheads_ref[...] = jnp.zeros_like(gheads_ref)

    conv_rows[CHUNK:, :] = conv_rows[0:16, :]

    if edge:

        @pl.when(i == chunks)
        def _():
            dx[...] = jnp.zeros_like(dx)
            gxbc_ref[:, XBC:] = jnp.zeros((CHUNK, SPLIT - XBC), bf16)

    @pl.when(i < chunks)
    def _():
        cum = cum_ref[...]
        step = step_ref[...]
        lead, kept, carried = decay_terms(start, c0, cum)
        b = act_ref[:, INNER : INNER + NSTATE]
        c = act_ref[:, INNER + NSTATE :]
        s_at = iota((CHUNK, CHUNK), 0)
        t_at = iota((CHUNK, CHUNK), 1)
        same = (c0 + s_at >= row_ref[0:1, :]) & (s_at <= t_at)
        scores = jnp.where(same, mm_nt(b, c), 0.0)
        log2 = cum * LOG2E
        log2_turned = log2.T
        step_two = two_parts(step)
        lead_two = two_parts(lead)
        kept_two = two_parts(kept)
        carried_two = two_parts(jnp.broadcast_to(carried, (16, LANES)))
        low_half = iota((CHUNK, LANES), 1) < HEADDIM
        c_turned = c.astype(f32).T.astype(bf16)
        g_scores = jnp.zeros((CHUNK, CHUNK), f32)
        gb = jnp.zeros((CHUNK, NSTATE), f32)
        gc = jnp.zeros((CHUNK, NSTATE), f32)
        for_step = jnp.zeros((CHUNK, LANES), f32)
        for_skip = jnp.zeros((CHUNK, LANES), f32)
        for_cum = jnp.zeros((CHUNK, LANES), f32)
        at_end = jnp.zeros((16, LANES), f32)

        def decay(head):
            gap = log2_turned[head : head + 1, :] - log2[:, head : head + 1]
            return jnp.exp2(jnp.minimum(gap, 0.0))

        for first in range(0, INNER, WIDE):
            cols = slice(first, first + WIDE)
            spread = spread_ref[:, cols]
            gather = gather_ref[cols, :]
            x = act_ref[:, cols].astype(f32)
            gm = gm_ref[:, cols]
            gm_f = gm.astype(f32)
            step_wide = mm(step_two, spread)
            lead_wide = mm(lead_two, spread)
            kept_wide = mm(kept_two, spread)
            carried_wide = mm(carried_two, spread)[0:1, :]
            stepped = x * step_wide
            stepped_low = stepped.astype(bf16)
            p = adjoint[:, cols]
            p_low = p.astype(bf16)
            s_next = later[:, cols].astype(f32)
            s_here = begin_ref[0, :, cols].astype(f32) + factor_ref[0, 0:1, cols] * enter_ref[:, cols].astype(f32)
            s_low = s_here.astype(bf16)
            later[:, cols] = s_low
            ends = jnp.sum((s_next * p).reshape(NSTATE // 16, 16, WIDE), axis=0)
            at_end = at_end + head_sum(ends, gather)
            intra = []
            for part in range(2):
                head = first // HEADDIM + 2 * part
                half = slice(part * LANES, (part + 1) * LANES)
                gm_pair = gm[:, half]
                x_pair = stepped_low[:, half]
                zero = jnp.zeros_like(x_pair)
                d0, d1 = decay(head), decay(head + 1)
                w = jnp.concatenate([(scores * d0).astype(bf16), (scores * d1).astype(bf16)], axis=1)
                blocks = jnp.concatenate(
                    [jnp.where(low_half, gm_pair, zero), jnp.where(low_half, zero, gm_pair)], axis=0
                )
                intra.append(mm(w, blocks))
                x_blocks = jnp.concatenate(
                    [jnp.where(low_half, x_pair, zero), jnp.where(low_half, zero, x_pair)], axis=0
                )
                gw = mm_nt(x_blocks, gm_pair)
                g_scores = g_scores + gw[:CHUNK] * d0 + gw[CHUNK:] * d1
            g_stepped = jnp.concatenate(intra, axis=1) + kept_wide * mm(b, p_low)
            dx[:, cols] = step_wide * g_stepped + skip_ref[:, cols] * gm_f
            for_step = for_step + head_sum(x * g_stepped, gather)
            for_cum = for_cum + head_sum(stepped_low.astype(f32) * g_stepped, gather)
            for_skip = for_skip + head_sum(x * gm_f, gather)
            gm_led = (lead_wide * gm_f).astype(bf16)
            gc = gc + mm_nt(gm_led, s_low)
            gb = gb + mm_nt((kept_wide * stepped).astype(bf16), p_low)
            adjoint[:, cols] = carried_wide * p + mm(c_turned, gm_led)

        g_scores = jnp.where(same, g_scores, 0.0)
        gb = gb + mm(g_scores.astype(bf16), c)
        gc = gc + mm(g_scores.T.astype(bf16), b)
        dx[:, INNER : INNER + NSTATE] = gb
        dx[:, INNER + NSTATE :] = gc
        skip_row = heads_ref[2:3, :]
        g_cum = rows_ref[...] - skip_row * for_skip - for_cum
        end_row = jnp.sum(at_end, axis=0, keepdims=True)
        g_cum = g_cum + jnp.where(iota((CHUNK, LANES), 0) == CHUNK - 1, end_row, 0.0)
        g_log = three_sum(mm(tri(False), three_parts(g_cum)))
        rate = heads_ref[1:2, :]
        g_step = for_step - rate * g_log
        raw = xbc_ref[:, XBC:].astype(f32) + heads_ref[0:1, :]
        g_raw = g_step * sigmoid(raw)
        g_raw = jnp.where(iota(g_raw.shape, 1) < HEADS, g_raw, 0.0)
        gxbc_ref[:, XBC:] = g_raw.astype(bf16)
        gheads_ref[0:8, :] += jnp.sum(g_raw.reshape(CHUNK // 8, 8, LANES), axis=0)
        gheads_ref[8:16, :] += jnp.sum((g_log * (-step * rate)).reshape(CHUNK // 8, 8, LANES), axis=0)
        gheads_ref[16:24, :] += jnp.sum(for_skip.reshape(CHUNK // 8, 8, LANES), axis=0)

    shifts = conv_shifts(start, c0)
    rows = (CHUNK, CHUNK + 16)
    s_at = iota(rows, 0)
    t_at = iota(rows, 1)
    reach = jnp.concatenate([row_ref[0:1, :], row_next_ref[0:1, :16]], axis=1) <= c0 + s_at
    turns = [((t_at == s_at + 3 - k) & reach).astype(bf16) for k in range(3)]
    for first in range(0, XBC, WIDE):
        cols = slice(first, first + WIDE)
        g = dx[:, cols] * slope_ref[:, cols].astype(f32)
        x = xbc_ref[:, cols]
        ext = jnp.concatenate([halo_ref[:, cols], x], axis=0)
        conv_rows[0:CHUNK, cols] = g.astype(bf16)
        g_ext = conv_rows[:, cols]
        total = taps_ref[3:4, cols] * g
        for k in range(3):
            total = total + taps_ref[k : k + 1, cols] * mm(turns[k], g_ext)
            part = (g * mm(shifts[k], ext)).reshape(CHUNK // 8, 8, WIDE)
            gtaps_ref[8 * k : 8 * k + 8, cols] += jnp.sum(part, axis=0)
        part = (g * x.astype(f32)).reshape(CHUNK // 8, 8, WIDE)
        gtaps_ref[24:32, cols] += jnp.sum(part, axis=0)
        gbias_ref[:, cols] += jnp.sum(g.reshape(CHUNK // 8, 8, WIDE), axis=0)
        gxbc_ref[:, cols] = total.astype(bf16)

    if not edge:

        @pl.when(i == last)
        def _():
            adjoint_out[...] = adjoint[...]
            later_out[...] = later[...]
            carry_out[...] = conv_rows[0:16, :]


def norm_back_kernel(
    place_ref, ggate_ref, gxbc_ref, gedge_ref, gw_ref, xw_ref, resid_ref, edge_ref, cot_ref, gain_ref,
    out_ref, out_edge_ref,
):
    gain = gain_ref[...]

    def back(g, resid):
        g = g * gain
        r = resid.astype(f32)
        scale = lax.rsqrt(jnp.mean(r * r, axis=1, keepdims=True) + norm_eps)
        n = r * scale
        return scale * (g - n * jnp.mean(g * n, axis=1, keepdims=True))

    @pl.when(pl.program_id(0) == 0)
    def _():
        out_edge_ref[...] = back(mm_nt(gedge_ref[...], xw_ref[...]), edge_ref[...])

    g = mm_nt(ggate_ref[...], gw_ref[...]) + mm_nt(gxbc_ref[...], xw_ref[...])
    out_ref[...] = cot_ref[...].astype(f32) + back(g, resid_ref[...])


def split_two(v):
    first = v.astype(bf16)
    return first, (v - first.astype(f32)).astype(bf16)


CUTS = [slice(i, i + 256) for i in range(0, D, 256)]


def symmetric(products, finish):
    for cut in CUTS:
        column = products(slice(0, cut.stop), cut)
        for at in CUTS:
            if at.start < cut.start:
                block = column[at]
                finish(at, cut, block)
                finish(cut, at, block.T)
        finish(cut, cut, column[cut])


def keep_left(ref, at, cut, first, second):
    for k, part in enumerate((first, first, second)):
        ref[at, slice(k * D + cut.start, k * D + cut.stop)] = part


def keep_right(ref, at, cut, first, second):
    for k, part in enumerate((first, second, first)):
        ref[slice(k * D + at.start, k * D + at.stop), cut] = part


def sweep(rows, gram_right, poly_right, poly_left, turn_left, gram):
    c1, c2, c3 = schulz_coef

    def polynomial(k, squared):
        right = poly_right.at[k]

        def keep(at, cut, block):
            p = c2 * gram[at, cut] + c3 * block
            if at == cut:
                p = p + jnp.where(iota(p.shape, 0) == iota(p.shape, 1), c1, 0.0)
            first, second = split_two(p)
            keep_left(poly_left, at, cut, first, second)
            keep_right(right, at, cut, first, second)

        symmetric(squared, keep)

    def one_sweep(k, _):
        polynomial(k, lambda at, cut: mm(gram_right[at, :], gram_right[:D, cut]))
        right = poly_right.at[k]

        def keep_turned(at, cut, t):
            keep_left(turn_left, at, cut, *split_two(t))

        def keep_gram(at, cut, a):
            gram[at, cut] = a
            keep_right(gram_right, at, cut, *split_two(a))

        symmetric(lambda at, cut: mm(poly_left[at, :], gram_right[:, cut]), keep_turned)
        symmetric(lambda at, cut: mm(turn_left[at, :], right[:, cut]), keep_gram)
        return 0

    lax.fori_loop(0, SWEEPS - 2, one_sweep, 0)
    k = SWEEPS - 2
    for cut in CUTS:
        for at in CUTS:
            keep_left(turn_left, at, cut, gram_right[at, cut], gram_right[slice(D + at.start, D + at.stop), cut])
    polynomial(k, lambda at, cut: mm(turn_left[at, :], gram_right[:, cut]))

    def times(r, right):
        first, second = split_two(r)
        return mm(jnp.concatenate([first, first, second], axis=1), right[...])

    def poly(r, k):
        return times(r, poly_right.at[k])

    def last_gram(r):
        k = SWEEPS - 2
        return poly(times(poly(r, k), gram_right), k)

    once = last_gram(rows)
    rows = c1 * rows + c2 * once + c3 * last_gram(once)
    for k in reversed(range(SWEEPS - 1)):
        rows = poly(rows, k)
    return rows


def start_sweeps(products, gram, gram_right):
    def keep(at, cut, block):
        gram[at, cut] = block

    symmetric(products, keep)
    trace = jnp.zeros((1, 1), f32)
    for cut in CUTS:
        g = gram[cut, cut]
        eye = iota(g.shape, 0) == iota(g.shape, 1)
        trace = trace + jnp.sum(jnp.sum(jnp.where(eye, g, 0.0), axis=1, keepdims=True), axis=0, keepdims=True)
    norm = jnp.sqrt(trace) + ortho_eps
    scale = 1.0 / (norm * norm)
    for cut in CUTS:
        a = gram[cut, :] * scale
        gram[cut, :] = a
        keep_right(gram_right, cut, slice(0, D), *split_two(a))
    return norm


def edge_add_kernel(place_ref, grad_ref, extra_ref, out_ref):
    out_ref[...] = grad_ref[...] + extra_ref[...]


def sweeps_kernel(
    place_ref, gate_plane, gate_rest, top_plane, top_rest, bottom_plane, bottom_rest, x_plane, x_rest, turn,
    own_in_ref, other_in_ref, own_out_ref, other_out_ref, gains_ref,
    both, x, gram_right, poly_right, poly_left, turn_left, gram,
):
    core = place_ref[0]
    count = own_in_ref.shape[0]
    own_in_ref[...] = jnp.zeros_like(own_in_ref)
    other_in_ref[...] = jnp.zeros_like(other_in_ref)
    own_out_ref[...] = jnp.zeros_like(own_out_ref)
    other_out_ref[...] = jnp.zeros_like(other_out_ref)
    scratch = (gram_right, poly_right, poly_left, turn_left, gram)
    size = 32
    half = D // 2
    last = slice(SPLIT - LANES, SPLIT)
    gains_ref[...] = mm(turn[...], jnp.concatenate([x_plane[:, last], x_rest[:, last]], axis=0))

    @pl.when(core == 0)
    def _():
        both[:half, :], both[half:, :] = gate_plane[...], gate_rest[...]
        x[:half, :], x[half:, :] = x_plane[...], x_rest[...]
        end = x[:, last]
        x[:, last] = jnp.where(iota(end.shape, 1) < HEADS, end, jnp.zeros_like(end))
        norm = start_sweeps(
            lambda at, cut: mm_nt(both[at, :], both[cut, :]) + mm_nt(x[at, :], x[cut, :]), gram, gram_right
        )
        at = iota((2 * size, D), 0)
        rows = (jnp.where(at < size, at, at - size + half) == iota((2 * size, D), 1)).astype(f32)
        rows = (sweep(rows, *scratch) / norm).astype(bf16)
        left, right = mm(rows, both[...]), mm(rows, x[...])
        own_in_ref[:, :INNER] = left[:count]
        own_in_ref[:, INNER:] = right[:count, : PROJ - INNER]
        other_in_ref[:, :INNER] = left[size : size + count].astype(bf16)
        other_in_ref[:, INNER:] = right[size : size + count, : PROJ - INNER].astype(bf16)

    @pl.when(core == 1)
    def _():
        both[:half, :D], both[half:, :D] = top_plane[...], top_rest[...]
        both[:half, D:], both[half:, D:] = bottom_plane[...], bottom_rest[...]
        top, bottom = both.at[:, :D], both.at[:, D:]
        norm = start_sweeps(
            lambda at, cut: mm_tn(top[:, at], top[:, cut]) + mm_tn(bottom[:, at], bottom[:, cut]), gram, gram_right
        )
        rows = jnp.concatenate(
            [ref[at : at + size, :].astype(f32) for at in (0, half) for ref in (top, bottom)], axis=0
        )
        rows = sweep(rows, *scratch) / norm
        for part in range(2):
            target = (own_out_ref, other_out_ref)[part]
            for side in range(2):
                first = (2 * part + side) * size
                target[side * count : (side + 1) * count, :] = rows[first : first + count].astype(target.dtype)


def spec(shape, index=None):
    return pl.BlockSpec(shape, (lambda i, _: (0,) * len(shape)) if index is None else index)


PARTS = (3, 3, 2)


def call(kernel, scalars, grid, in_specs, out_specs, out_shape, scratch, cost, args, aliases={}):
    return pl.pallas_call(
        kernel,
        grid_spec=pltpu.PrefetchScalarGridSpec(
            num_scalar_prefetch=1,
            grid=grid,
            in_specs=in_specs,
            out_specs=out_specs,
            scratch_shapes=scratch,
        ),
        out_shape=[jax.ShapeDtypeStruct(s, t) for s, t in out_shape],
        input_output_aliases=aliases,
        cost_estimate=pl.CostEstimate(flops=cost[0], bytes_accessed=cost[1], transcendentals=0),
        compiler_params=pltpu.CompilerParams(
            dimension_semantics=("arbitrary",), vmem_limit_bytes=56 * 1024 * 1024
        ),
    )(scalars, *args)


def run_setup(docs, vec, tok):
    shapes = [
        ((tok, LANES), jnp.int32),
        ((8, tok + CHUNK), jnp.int32),
        ((LANES, INNER), bf16),
        ((INNER, LANES), bf16),
        ((CONV, XBC), f32),
        ((1, XBC), f32),
        ((8, LANES), f32),
        ((1, INNER), f32),
        ((1, INNER), f32),
        ((1, D), f32),
    ]
    return call(
        setup_kernel, docs, (1,), [spec(vec.shape)], [spec(s) for s, _ in shapes], shapes, [], (10**7, 10**6), (vec,)
    )


def run_states(place, start, spread, proj_x, taps, bias, heads, tok):
    chunks = tok // CHUNK
    halo = lambda i, _: (jnp.where(i == 0, tok // 16 + 7, 8 * i - 1), 0)
    rows = lambda i, _: (i, 0)
    return call(
        states_kernel,
        place,
        (chunks,),
        [
            spec((CHUNK, LANES), rows),
            spec((LANES, INNER)),
            spec((CHUNK, SPLIT), rows),
            spec((16, SPLIT), halo),
            spec((CONV, XBC)),
            spec((1, XBC)),
            spec((8, LANES)),
        ],
        [
            spec((CHUNK, XBC), rows),
            spec((CHUNK, XBC), rows),
            spec((CHUNK, LANES), rows),
            spec((CHUNK, LANES), rows),
            spec((CHUNK, LANES), rows),
            spec((1, NSTATE, INNER), lambda i, _: (i, 0, 0)),
            spec((1, 8, INNER), lambda i, _: (i, 0, 0)),
            spec((NSTATE + 16, INNER)),
        ],
        [
            ((tok, XBC), bf16),
            ((tok, XBC), bf16),
            ((tok, LANES), f32),
            ((tok, LANES), f32),
            ((tok, LANES), f32),
            ((chunks, NSTATE, INNER), bf16),
            ((chunks, 8, INNER), f32),
            ((NSTATE + 16, INNER), bf16),
        ],
        [pltpu.VMEM((NSTATE, INNER), f32), pltpu.VMEM((8, LANES), f32)],
        (10**6, 10**5),
        (start, spread, proj_x, proj_x, taps, bias, heads),
    )


def run_mix(place, start, spread, act, cum, step, begin, skip, tok):
    rows = lambda i, _: (i, 0)
    return call(
        mix_kernel,
        place,
        (tok // CHUNK,),
        [
            spec((CHUNK, LANES), rows),
            spec((LANES, INNER)),
            spec((CHUNK, XBC), rows),
            spec((CHUNK, LANES), rows),
            spec((CHUNK, LANES), rows),
            spec((1, NSTATE, INNER), lambda i, _: (i, 0, 0)),
            spec((1, INNER)),
        ],
        [spec((CHUNK, INNER), rows)],
        [((tok, INNER), f32)],
        [],
        (10**6, 10**5),
        (start, spread, act, cum, step, begin, skip),
    )[0]


def run_gate(order, mixed, gate, act, lead, enter, resid, cot, weights, gain, tok):
    block = 2 * CHUNK
    rows = lambda i, _: (i, 0)
    return call(
        gate_kernel,
        order,
        (tok // block,),
        [
            spec((block, INNER), rows),
            spec((block, INNER), rows),
            spec((block, NSTATE), lambda i, _: (i, (INNER + NSTATE) // NSTATE)),
            spec((block, LANES), rows),
            spec((NSTATE, INNER)),
            spec((block, D), rows),
            spec((block, D), rows),
            spec((D, D), lambda i, _: (0, INNER // D)),
            spec((D, D), lambda i, _: (0, INNER // D + 1)),
            spec((1, INNER)),
        ],
        [
            spec((block, D), rows),
            spec((block, INNER), rows),
            spec((block, INNER), rows),
            spec((block, LANES), rows),
            spec((D // 2, INNER)),
            spec((D // 2, INNER)),
            spec((NSTATE, INNER)),
            spec((8, INNER)),
        ],
        [
            ((tok, D), bf16),
            ((tok, INNER), bf16),
            ((tok, INNER), bf16),
            ((tok, LANES), f32),
            ((D // 2, INNER), bf16),
            ((D // 2, INNER), bf16),
            ((NSTATE, INNER), bf16),
            ((8, INNER), f32),
        ],
        [
            pltpu.VMEM((block, INNER), f32),
            pltpu.VMEM((block, INNER), f32),
            pltpu.VMEM((block, INNER), bf16),
            pltpu.VMEM((block, INNER), f32),
            pltpu.VMEM((NSTATE, INNER), f32),
            pltpu.VMEM((INNER, D), f32),
            pltpu.VMEM((INNER, D), bf16),
        ],
        (10**6, 10**5),
        (mixed, gate, act, lead, enter, resid, cot, weights, weights, gain),
    )


def run_back(place, start, start_row, spread, gather, proj_x, act, slope, cum, step, rows_sum, gmixed, begin, factor, enter, taps, heads, skip, state, gxbc, token, part, count, tok):
    chunks = tok // CHUNK
    edge = part == count
    at = lambda i: jnp.maximum(part - 1 - i, part - count)
    rows = lambda i, _: (at(i), 0)
    halo = lambda i, _: (jnp.where(at(i) == 0, tok // 16 + 7, 8 * at(i) - 1), 0)
    cube = lambda i, _: (at(i), 0, 0)
    anywhere = pl.BlockSpec(memory_space=pl.ANY)
    args = (start, start_row, start_row, spread, gather, proj_x, proj_x, act, slope, cum, step, rows_sum, gmixed, begin, factor, enter, taps, heads, skip, *state, token)
    specs = [
        spec((CHUNK, LANES), rows),
        spec((8, CHUNK), lambda i, _: (0, at(i))),
        spec((8, CHUNK), lambda i, _: (0, jnp.where(i == count, 0, at(i) + 1))),
        spec((LANES, INNER)),
        spec((INNER, LANES)),
        spec((CHUNK, SPLIT), rows),
        spec((16, SPLIT), halo),
        spec((CHUNK, XBC), rows),
        spec((CHUNK, XBC), rows),
        spec((CHUNK, LANES), rows),
        spec((CHUNK, LANES), rows),
        spec((CHUNK, LANES), rows),
        spec((CHUNK, INNER), rows),
        spec((1, NSTATE, INNER), cube),
        spec((1, 8, INNER), cube),
        spec((NSTATE, INNER)),
        spec((CONV, XBC)),
        spec((8, LANES)),
        spec((1, INNER)),
        spec((NSTATE, INNER)),
        spec((NSTATE, INNER)),
        spec((16, XBC)),
        anywhere,
    ]
    aliases = {}
    if gxbc is not None:
        args, specs = args + (gxbc,), specs + [anywhere]
        aliases = {len(args): 0}
    out = call(
        functools.partial(back_kernel, part, edge),
        place,
        (count + (1 if edge else 0),),
        specs,
        [
            spec((CHUNK, SPLIT), lambda i, _: (jnp.where(i == count, chunks, at(i)), 0)),
            spec((8 * CONV, XBC)),
            spec((8, XBC)),
            spec((24, LANES)),
            spec((NSTATE, INNER)),
            spec((NSTATE, INNER)),
            spec((16, XBC)),
        ],
        [
            ((tok + CHUNK, SPLIT), bf16),
            ((8 * CONV, XBC), f32),
            ((8, XBC), f32),
            ((24, LANES), f32),
            ((NSTATE, INNER), f32),
            ((NSTATE, INNER), bf16),
            ((16, XBC), bf16),
        ],
        [
            pltpu.VMEM((NSTATE, INNER), f32),
            pltpu.VMEM((NSTATE, INNER), bf16),
            pltpu.VMEM((CHUNK + 16, XBC), bf16),
            pltpu.VMEM((CHUNK, XBC), f32),
        ],
        (10**6, 10**5),
        args,
        aliases,
    )
    return out[0], out[1:4], out[4:]


def run_norm_back(place, ggate, gxbc, gate_w, x_w, resid, edge, cot, gain, tok):
    block = 2 * CHUNK
    rows = lambda i, _: (i, 0)
    return call(
        norm_back_kernel,
        place,
        (tok // block,),
        [
            spec((block, INNER), rows),
            spec((block, SPLIT), rows),
            spec((16, SPLIT), lambda i, _: (tok // 16 + 7, 0)),
            spec((D, INNER)),
            spec((D, SPLIT)),
            spec((block, D), rows),
            spec((16, D)),
            spec((block, D), rows),
            spec((1, D)),
        ],
        [spec((block, D), rows), spec((16, D))],
        [((tok, D), f32), ((16, D), f32)],
        [],
        (10**6, 10**5),
        (ggate, gxbc, gxbc, gate_w, x_w, resid, edge, cot, gain),
    )


SWEEP_SCRATCH = [
    pltpu.VMEM((3 * D, D), bf16),
    pltpu.VMEM((SWEEPS - 1, 3 * D, D), bf16),
    pltpu.VMEM((D, 3 * D), bf16),
    pltpu.VMEM((D, 3 * D), bf16),
    pltpu.VMEM((D, D), f32),
]


def run_edge_add(place, grad, extra, tok):
    at = spec((16, D), lambda i, _: (tok // 16 - 1, 0))
    return call(
        edge_add_kernel, place, (1,), [at, spec((16, D))], [at], [((tok, D), f32)], [], (10**5, 10**5), (grad, extra), {1: 0}
    )[0]


def run_sweeps(core, both, x, turn, in_shape, out_shape):
    half = D // 2
    return call(
        sweeps_kernel,
        core,
        (1,),
        [spec((half, INNER))] * 2
        + [spec((half, D), lambda i, _: (0, INNER // D))] * 2
        + [spec((half, D), lambda i, _: (0, INNER // D + 1))] * 2
        + [spec((half, SPLIT))] * 2
        + [spec((D, D))],
        [spec(in_shape), spec(in_shape), spec(out_shape), spec(out_shape), spec((D, LANES))],
        [(in_shape, f32), (in_shape, bf16), (out_shape, f32), (out_shape, bf16), ((D, LANES), f32)],
        [pltpu.VMEM((D, INNER), bf16), pltpu.VMEM((D, SPLIT), bf16)] + SWEEP_SCRATCH,
        (30 * 10**9, 10**7),
        (*both, *both, *both, *x, turn),
    )


class Crossing:
    def __init__(self, payload, forward):
        self.forward = forward
        self.payload = payload
        self.near = self.hop(payload, [(0, 1), (2, 3)])

    def hop(self, v, pairs):
        return lax.ppermute(v, "seq", [(a, b) if self.forward else (3 - a, 3 - b) for a, b in pairs])

    def second(self):
        state, near = (p[:NSTATE].astype(f32) for p in (self.payload, self.near))
        both = (state + decay_of(self.payload) * near).astype(bf16)
        self.over = self.hop(both, [(1, 2)])
        return both

    def third(self):
        self.far = self.hop(self.over, [(2, 3)])
        return self.over

    def result(self):
        near = self.near[:NSTATE].astype(f32)
        return near + self.over.astype(f32) + decay_of(self.near) * self.far.astype(f32)


class Grid:
    def __init__(self):
        self.dp = lax.axis_size("dp")
        self.nz = self.dp // 2
        seq, dp = lax.axis_index("seq"), lax.axis_index("dp")
        self.x, self.core, self.z, self.y = seq // 2, seq % 2, dp // 2, dp % 2

    def number(self, x, core, z, y):
        return (x * 2 + core) * self.dp + (z % self.nz) * 2 + y

    def hop(self, v, move):
        pairs = [
            (self.number(x, c, z, y), self.number(*move(x, c, z, y)))
            for x in range(2)
            for c in range(2)
            for z in range(self.nz)
            for y in range(2)
        ]
        return lax.ppermute(v, ("seq", "dp"), pairs)

    def to_odd(self, v):
        return lax.ppermute(v, "seq", [(0, 1), (2, 3)])

    def to_even(self, v):
        return lax.ppermute(v, "seq", [(1, 0), (3, 2)])

    def to_core(self, v):
        return self.hop(v, lambda x, c, z, y: (x, 1 - c, z, y))

    def to_near(self, v):
        return self.hop(v, lambda x, c, z, y: (x, c, z, 1 - y) if c == 0 else (1 - x, c, z, y))

    def to_far(self, v):
        return self.hop(v, lambda x, c, z, y: (1 - x, c, z, y) if c == 0 else (x, c, z, 1 - y))

    def to_diagonal(self, v):
        return self.hop(v, lambda x, c, z, y: (1 - x, c, z, 1 - y))

    def to_z(self, v, k):
        return self.hop(v, lambda x, c, z, y: (x, c, z + k, y))

    def added(self, own, other):
        return (own.astype(f32) + other.astype(f32)).astype(bf16)

    def scatter_core(self, own, other, later=None):
        other = self.to_core(other)
        return self.added(own, other if later is None else after(other, later))

    def scatter_far(self, v, later=None):
        half = v.shape[0] // 2
        other = self.to_far(v[half:])
        return self.added(v[:half], other if later is None else after(other, later))

    def scatter_near(self, v, later=None):
        half = v.shape[0] // 2
        other = self.to_near(v[half:])
        return self.added(v[:half], other if later is None else after(other, later))

    def scatter_z(self, v, later=None):
        part = v.shape[0] // self.nz
        others = [self.to_z(v[k * part : (k + 1) * part], -k) for k in range(1, self.nz)]
        if later is not None:
            others = after(others, later)
        return sum([other.astype(f32) for other in others], v[:part].astype(f32))

    def gather_z(self, v, later=None):
        parts = [self.to_z(v, k) for k in range(1, self.nz)]
        if later is not None:
            parts = after(parts, later)
        return jnp.concatenate([v] + parts, axis=0)

    def gather_near(self, v, later=None):
        other = self.to_near(v)
        return jnp.concatenate([v, other if later is None else after(other, later)], axis=0)

    def gather_far(self, v):
        return jnp.concatenate([v, self.to_far(v)], axis=0)

    def gather_core(self, v):
        return jnp.concatenate([v, self.to_core(v)], axis=0)

    def order(self, rows):
        at = jnp.arange(8 * self.nz * rows)
        block, row = at // rows, at % rows
        k, near, far, other = block % self.nz, block // self.nz % 2, block // (2 * self.nz) % 2, block // (4 * self.nz)
        core = self.core ^ other
        dx, dy = jnp.where(core == 0, far, near), jnp.where(core == 0, near, far)
        return self.number(self.x ^ dx, core, self.z - k, self.y ^ dy) * rows + row

    def turner(self, rows):
        order = self.order(rows)
        return (jnp.arange(order.shape[0])[:, None] == order[None, :]).astype(bf16)

    def sum_steps(self):
        return [(axis, 1 << bit) for axis in ("seq", "dp") for bit in range((lax.axis_size(axis) - 1).bit_length())]

    def sum_step(self, v, axis, step):
        return v + lax.ppermute(v, axis, [(i, i ^ step) for i in range(lax.axis_size(axis))])


def after(v, *others):
    return lax.optimization_barrier((v, *others))[0]


def beside(gate, out):
    count = gate.shape[0]
    return jnp.concatenate([gate, out[:count], out[count:]], axis=1)


def stacked(pair, count):
    blocks = pair.reshape(-1, count, 2, D)
    return jnp.moveaxis(blocks, 2, 1).reshape(-1, D)


def decay_of(payload):
    return payload[NSTATE : NSTATE + 1].astype(f32) + payload[NSTATE + 1 : NSTATE + 2].astype(f32)


def per_device(
    resid,
    cotangent,
    doc_lengths,
    in_weight,
    out_weight,
    vec_params,
    in_moment,
    out_moment,
    vec_first,
    vec_second,
):
    gain_in = vec_params[:D]
    place = lax.axis_index("seq")
    tok = resid.shape[1]
    first_token = jnp.reshape(place * tok, (1,)).astype(jnp.int32)
    docs = jnp.concatenate([first_token, doc_lengths[0].astype(jnp.int32)])

    grid = Grid()
    count = in_weight.shape[0]
    order = grid.order(1).astype(jnp.int32)
    x_local = jnp.pad(in_weight[:, INNER:].astype(bf16), ((0, 0), (0, SPLIT + INNER - PROJ)))
    both_local = beside(in_weight[:, :INNER], out_weight).astype(bf16)
    start, start_row, spread, gather, conv_taps, bias, heads, skip, gain, gain_row = run_setup(
        docs, after(vec_params[None, :], x_local), tok
    )
    x_line = grid.gather_z(x_local, (start, both_local))
    edge = passed_along(after(resid[0, tok - 16 :], x_line), "seq", 1)
    in_turn = grid.turner(count)
    x_pair = grid.gather_near(x_line)
    both_from = after(both_local, x_pair)
    x_plane = grid.gather_far(after(x_pair, in_turn))
    rows = jnp.concatenate([resid[0], jnp.zeros((CHUNK - 16, D), bf16), edge], axis=0).astype(f32)
    normed = mm(in_norm(rows, gain_in).astype(bf16), in_turn).astype(bf16)
    x_rel = grid.gather_core(after(x_plane, normed))
    proj_x = mm(normed, x_rel).astype(bf16)
    act, slope, cum, step, lead, begin, factor, end = run_states(
        first_token, start, spread, proj_x, conv_taps, bias, heads, tok
    )
    entering = Crossing(end, True)
    both_line = grid.gather_z(both_from, end)
    x_w = mm(after(in_turn, both_line, end), x_rel).astype(bf16)
    both_pair = grid.gather_near(both_line, x_w)
    both_plane = grid.gather_far(both_pair)
    over = entering.second()
    mixed = run_mix(first_token, start, spread, act, cum, after(step, entering.over, x_w, both_pair), begin, skip, tok)
    over = entering.third()
    both_rel = grid.gather_core(after(both_plane, mixed))
    gate = mm(after(normed, mixed, over)[:tok], both_rel[:, :INNER]).astype(bf16)
    enter = entering.result().astype(bf16)
    placed = count % 8 == 0
    placing = both_rel
    if not placed:
        out_turn = grid.turner(2 * count)
        out_nat = mm(out_turn, stacked(both_rel[:, INNER:], count)).astype(bf16)
        placing = jnp.concatenate([both_rel[:, :INNER], out_nat[:D], out_nat[D:]], axis=1)
    block_out, gmixed, ggate, rows_sum, out_own, out_other, gstate, ggain_norm = run_gate(
        order, mixed, gate, act, lead, enter, resid[0], cotangent[0], placing, gain, tok
    )
    half = D // 2
    if not placed:
        whole = jnp.concatenate(
            [jnp.concatenate([out_own[:, c], out_other[:, c]], axis=0) for c in (slice(0, D), slice(D, None))], axis=0
        )
        whole = mm_tn(out_turn, whole).astype(bf16).reshape(-1, 2, count, D)
        whole = jnp.concatenate([whole[:, 0].reshape(-1, D), whole[:, 1].reshape(-1, D)], axis=1)
        out_own, out_other = whole[:half], whole[half:]
    leaving = Crossing(jnp.concatenate([gstate, end[NSTATE:]], axis=0), False)
    gate_other = mm_tn(normed[:tok, half:], ggate).astype(bf16)
    over = leaving.second()
    both_other = jnp.concatenate([after(gate_other, over), out_other], axis=1)
    leaving.third()
    both_other = after(both_other, leaving.far)
    gate_own = mm_tn(after(normed, leaving.far)[:tok, :half], ggate).astype(bf16)
    both_own = jnp.concatenate([gate_own, out_own], axis=1)
    gate_w = mm(after(in_turn, leaving.far), both_rel[:, :INNER]).astype(bf16)
    both_sum = grid.scatter_core(both_own, both_other, gate_w)
    final = (end[:NSTATE].astype(f32) + decay_of(end) * enter.astype(f32)).astype(bf16)
    state = (after(leaving.result(), both_sum), final, jnp.zeros((16, XBC), bf16))
    gxbc = None
    sums = []
    part = tok // CHUNK
    for size, stage in zip(PARTS, (grid.scatter_far, grid.scatter_near, grid.scatter_z)):
        gxbc, part_sums, state = run_back(
            first_token, start, start_row, spread, gather, proj_x, act, slope, cum, step, rows_sum, gmixed, begin, factor,
            enter, conv_taps, heads, skip, state, gxbc, both_sum, part, size, tok,
        )
        part = part - size
        sums.append(part_sums)
        both_sum = stage(both_sum, part_sums[2])
    gtaps, gbias, gheads = [sum(s[1:], s[0]) for s in zip(*sums)]
    x_other = mm_tn(normed[:, half:], gxbc).astype(bf16)
    both_sum = after(both_sum, x_other)
    gate_moment = moment_decay * in_moment[:, :INNER] + both_sum[:, :INNER]
    out_moment_new = moment_decay * out_moment + stacked(both_sum[:, INNER:], count)
    both_moment = beside(gate_moment, out_moment_new).astype(bf16)
    x_own = mm_tn(after(normed, x_other)[:, :half], gxbc).astype(bf16)
    x_sum = grid.scatter_core(x_own, x_other)
    x_half = grid.scatter_far(x_sum)
    gtaps, gbias, gheads, ggain_norm = after((gtaps, gbias, gheads, ggain_norm), x_sum)
    head_sums = jnp.sum(gheads.reshape(3, 8, LANES), axis=1)[:, :HEADS]
    vec_grad = jnp.concatenate(
        [
            jnp.sum(ggain_norm, axis=0),
            jnp.sum(gtaps.reshape(CONV, 8, XBC), axis=1).reshape(-1),
            jnp.sum(gbias, axis=0),
            head_sums.reshape(-1),
        ]
    )
    x_sum = grid.scatter_near(after(x_half, vec_grad))
    both_line = grid.gather_z(both_moment, x_sum)
    vec_grad = grid.sum_step(after(vec_grad, x_sum), "seq", 1)
    both_pair = grid.gather_near(both_line)
    x_grad = after(grid.scatter_z(x_sum), vec_grad, both_pair)[:, : PROJ - INNER]
    x_moment = moment_decay * in_moment[:, INNER:] + x_grad
    in_moment_new = jnp.concatenate([gate_moment, x_moment], axis=1)
    device = grid.number(grid.x, grid.core, grid.z, grid.y)
    weight_low = in_weight.astype(bf16).astype(f32)
    gain_sum = jnp.sum(both_sum[:, :INNER] * weight_low[:, :INNER], axis=1, keepdims=True)
    gain_sum = gain_sum + jnp.sum(x_grad * weight_low[:, INNER:], axis=1, keepdims=True)
    gain_sum = gain_sum / lax.dynamic_slice(gain_in, (device * count,), (count,))[:, None]
    first = gain_sum.astype(bf16).astype(f32)
    second = (gain_sum - first).astype(bf16).astype(f32)
    third = gain_sum - first - second
    lane = jnp.arange(SPLIT)[None, :] - (PROJ - INNER)
    x_moment = jnp.pad(x_moment, ((0, 0), (0, SPLIT + INNER - PROJ)))
    for k, part in enumerate((first, second, third)):
        x_moment = jnp.where(lane == k, part, x_moment)
    x_moment = x_moment.astype(bf16)
    both_plane = grid.gather_far(after(both_pair, x_moment))
    x_line = grid.gather_z(x_moment)
    x_pair = grid.gather_near(x_line)
    line_steps = [1 << bit for bit in range(1, (grid.dp - 1).bit_length())]
    vec_grad = after(vec_grad, x_line)
    for step_size in line_steps[:-1]:
        vec_grad = grid.sum_step(vec_grad, "dp", step_size)
    x_pair = after(x_pair, vec_grad, both_plane)
    input_grad, edge_grad = run_norm_back(
        first_token, ggate, after(gxbc, x_pair), gate_w, x_w, resid[0], edge, cotangent[0], gain_row, tok
    )
    vec_grad = grid.sum_step(after(vec_grad, x_pair), "dp", line_steps[-1])
    x_plane = after(grid.gather_far(x_pair), edge_grad, vec_grad)
    both_rest = grid.to_core(after(both_plane, x_pair))
    extra = passed_along(edge_grad, "seq", -1)
    x_rest = grid.to_core(x_plane)
    vec_grad = grid.sum_step(grid.sum_step(after(vec_grad, x_plane), "seq", 2), "dp", 1)
    input_grad = run_edge_add(first_token, input_grad, after(extra, x_plane), tok)
    own_in, other_in, own_out, other_out, gains = run_sweeps(
        jnp.reshape(grid.core, (1,)), (both_plane, both_rest), (x_plane, x_rest), after(in_turn, vec_grad, input_grad), in_weight.shape, out_weight.shape
    )
    at = PROJ - INNER - (SPLIT - LANES)
    vec_grad = jnp.concatenate([jnp.sum(gains[:, at : at + 3], axis=1), vec_grad])
    even = grid.core == 0
    in_orth = jnp.where(even, own_in, grid.to_odd(other_in).astype(f32))
    out_orth = jnp.where(even, grid.to_even(other_out).astype(f32), own_out)
    in_weight_new = (
        in_weight * (1.0 - muon_rate * muon_shrink) - muon_rate * math.sqrt(PROJ / D) * in_orth
    )
    out_weight_new = out_weight * (1.0 - muon_rate * muon_shrink) - muon_rate * out_orth
    first_new = adam_first * vec_first + (1.0 - adam_first) * vec_grad
    second_new = adam_second * vec_second + (1.0 - adam_second) * vec_grad * vec_grad
    first_hat = first_new / (1.0 - adam_first**STEP)
    second_hat = second_new / (1.0 - adam_second**STEP)
    params_new = vec_params - adam_rate * first_hat / (jnp.sqrt(second_hat) + adam_eps)
    return (
        block_out[None],
        input_grad[None],
        in_moment_new,
        in_weight_new,
        out_moment_new,
        out_weight_new,
        first_new,
        second_new,
        params_new,
    )


def solution(mesh):
    return jax.shard_map(
        per_device,
        mesh=mesh,
        in_specs=(
            P("dp", "seq", None),
            P("dp", "seq", None),
            P("dp", None),
            P(("seq", "dp"), None),
            P(("seq", "dp"), None),
            P(),
            P(("seq", "dp"), None),
            P(("seq", "dp"), None),
            P(),
            P(),
        ),
        out_specs=(
            P("dp", "seq", None),
            P("dp", "seq", None),
            P(("seq", "dp"), None),
            P(("seq", "dp"), None),
            P(("seq", "dp"), None),
            P(("seq", "dp"), None),
            P(),
            P(),
            P(),
        ),
        check_vma=False,
    )
```
